512 devices in a mesh: ctx: 64 (over x, z, core), grp: 8 (over y).
Axes of the slice: x: 4, y: 8, z: 8, core: 2. Of those that a mesh axis runs over, the one named last changes fastest.
Arguments:
- queries: bfloat16 [131072, 2560], P(('ctx', 'grp')), may hold values from -40 to 40
- key_value_rows: bfloat16 [131072, 1024], P(('ctx', 'grp')), may hold values from -20 to 20
- unit_slot: int32 [256], replicated, may hold values from 0 to 255, as said below
- unit_doc: int32 [256], replicated, may hold values from 0 to 127, as said below
Outputs:
- attended: bfloat16 [131072, 2560], P(('ctx', 'grp'))
The draws below stay inside these ranges and needn't reach their ends.
Inputs may be any that keep to these rules, and one draw needn't show every extreme that they name: `unit_slot`: A permutation of the slots; the units of one document, in stream order, take consecutive slots of one aligned block of 4 slots, and each block is filled by whole documents. `unit_doc`: starts at 0 and rises by one where a new document begins; a document holds 1 to 4 units.
All inputs are finite; a program needn't handle non-finite values.
Results may differ from the reference program's by a relative error of at most 0.007.
Values may be sent and summed in bfloat16 or wider, within the bound.
A program may use at most 64 MiB of HBM per device.

```python
import math
import jax
import jax.numpy as jnp
from jax import lax

QUERY_HEADS = 20
KEY_VALUE_HEADS = 4
HEAD_SIZE = 128
DEVICE_TOKENS = 256
TOKEN_ROWS = 131072
UNITS_GRP = 4
N_CTX = 64
N_GRP = 8


def stream_layout(key):
    slots = jnp.arange(DEVICE_TOKENS, dtype=jnp.int32)
    within_block = slots % UNITS_GRP
    shuffled = jax.random.permutation(jax.random.fold_in(key, 11), DEVICE_TOKENS).astype(jnp.int32)
    sort_keys = slots // UNITS_GRP * (DEVICE_TOKENS + 1) + jnp.where(within_block == 0, 0, shuffled + 1)
    order_in = jnp.argsort(sort_keys, stable=True).astype(jnp.int32)
    inverse = jnp.argsort(order_in, stable=True).astype(jnp.int32)
    rank_in = inverse % UNITS_GRP
    opens = jnp.where(rank_in < UNITS_GRP // 2, 1, 0).astype(jnp.int32)
    begin = lax.cummax(jnp.where(opens == 1, slots, 0), axis=0)
    within = slots - begin
    ranking = jax.random.permutation(jax.random.fold_in(key, 12), DEVICE_TOKENS).astype(jnp.int32)
    ordering = jnp.argsort(jnp.take(ranking, begin) * UNITS_GRP + within).astype(jnp.int32)
    first_flags = jnp.take(opens, ordering)
    return (ordering, (jnp.cumsum(first_flags) - 1).astype(jnp.int32))


def key_field(key, spread):
    row_width = 2 * KEY_VALUE_HEADS * HEAD_SIZE
    raw = jax.random.normal(key, (TOKEN_ROWS, row_width), jnp.float32)
    levels = jnp.exp(jax.random.uniform(jax.random.fold_in(key, 31), (TOKEN_ROWS, 1), jnp.float32, -spread, 1e-06))
    raw = raw * levels
    joined_pair = raw.reshape(TOKEN_ROWS // 2, 2, row_width)
    later_keys = joined_pair[:, 1, :KEY_VALUE_HEADS * HEAD_SIZE]
    second_half = jnp.concatenate([later_keys, joined_pair[:, 1, KEY_VALUE_HEADS * HEAD_SIZE:]], axis=1)
    return jnp.stack([joined_pair[:, 0], second_half], axis=1).reshape(TOKEN_ROWS, row_width)


def draw_unit_slot(key, part):
    ordering, documents = stream_layout(key)
    return ordering


def draw_unit_doc(key, part):
    ordering, documents = stream_layout(key)
    return documents


def draw_key_value_rows(key, part):
    score_field = key_field(key, 0.0)
    return jnp.clip(score_field, -20.0, 20.0).astype(jnp.bfloat16)


def draw_queries(key, part):
    key = jax.random.fold_in(key, 3)
    fresh = jax.random.normal(key, (TOKEN_ROWS, QUERY_HEADS * HEAD_SIZE), jnp.float32)
    return jnp.clip(fresh, -40.0, 40.0).astype(jnp.bfloat16)


def setup_inputs(seed: int = 0) -> dict:
    streams_of = jax.random.split(jax.random.key(seed), 5)
    return {
        "queries": draw_queries(jax.random.fold_in(streams_of[4], 71), 0),
        "key_value_rows": draw_key_value_rows(jax.random.fold_in(streams_of[4], 71), 0),
        "unit_slot": draw_unit_slot(jax.random.fold_in(streams_of[4], 71), 0),
        "unit_doc": draw_unit_doc(jax.random.fold_in(streams_of[4], 71), 0),
    }


minimum_score = -1e+30

def group_attention(query_token_rows, paired_token_rows, position, document):
    count_of_rows = query_token_rows.shape[0]
    query_per_key_heads = QUERY_HEADS // KEY_VALUE_HEADS
    inverse_root = 1.0 / math.sqrt(HEAD_SIZE)
    head_grouped = query_token_rows.astype(jnp.float32).reshape(count_of_rows, KEY_VALUE_HEADS, query_per_key_heads, HEAD_SIZE)
    key_head_rows = paired_token_rows[:, :KEY_VALUE_HEADS * HEAD_SIZE].astype(jnp.float32).reshape(count_of_rows, KEY_VALUE_HEADS, HEAD_SIZE)
    value_head_rows = paired_token_rows[:, KEY_VALUE_HEADS * HEAD_SIZE:].astype(jnp.float32).reshape(count_of_rows, KEY_VALUE_HEADS, HEAD_SIZE)
    allowed = (document[None, :] == document[:, None]) & (position[None, :] <= position[:, None])
    stacked = (jnp.transpose(head_grouped, (1, 0, 2, 3)), jnp.transpose(key_head_rows, (1, 0, 2)), jnp.transpose(value_head_rows, (1, 0, 2)))

    def one_head(head_parts):
        query_head, key_head, value_head = head_parts
        scores = jnp.einsum('qgd,kd->gqk', query_head, key_head) * inverse_root
        masked = jnp.where(allowed[None], scores, minimum_score)
        largest = lax.optimization_barrier(jnp.max(masked, axis=-1, keepdims=True))
        exponent = jnp.where(allowed[None], jnp.exp(scores - largest), 0.0)
        running_sum = lax.optimization_barrier(jnp.sum(exponent, axis=-1))
        weights = lax.optimization_barrier(exponent.astype(jnp.bfloat16)).astype(jnp.float32)
        summed = jnp.einsum('gqk,kd->qgd', weights, value_head)
        return summed / jnp.transpose(running_sum)[:, :, None]
    result = lax.map(one_head, stacked)
    return jnp.transpose(result, (1, 0, 2, 3)).reshape(count_of_rows, QUERY_HEADS * HEAD_SIZE).astype(jnp.bfloat16)

def reference(queries, key_value_rows, unit_slot, unit_doc):
    shards = N_CTX * N_GRP
    unit_count = DEVICE_TOKENS // N_CTX
    slot_unit = jnp.argsort(unit_slot).astype(jnp.int32)
    query_all = queries.reshape(N_CTX, N_GRP, DEVICE_TOKENS, QUERY_HEADS * HEAD_SIZE)
    pair_complete = key_value_rows.reshape(N_CTX, N_GRP, DEVICE_TOKENS, 2 * KEY_VALUE_HEADS * HEAD_SIZE)
    ctx_ids = jnp.arange(N_CTX, dtype=jnp.int32)
    grp_ids = jnp.arange(N_GRP, dtype=jnp.int32)

    def one_group(target):
        group_units = lax.dynamic_slice_in_dim(slot_unit, target * unit_count, unit_count)
        query_token_rows = jnp.take(query_all, group_units, axis=2)
        paired_token_rows = jnp.take(pair_complete, group_units, axis=2)
        position = group_units[None, None, :] * shards + ctx_ids[:, None, None] * N_GRP + grp_ids[None, :, None]
        document = jnp.take(unit_doc, group_units)[None, None, :] + 0 * position
        query_token_rows = jnp.transpose(query_token_rows, (1, 0, 2, 3)).reshape(N_GRP * DEVICE_TOKENS, QUERY_HEADS * HEAD_SIZE)
        paired_token_rows = jnp.transpose(paired_token_rows, (1, 0, 2, 3)).reshape(N_GRP * DEVICE_TOKENS, 2 * KEY_VALUE_HEADS * HEAD_SIZE)
        position = jnp.transpose(position, (1, 0, 2)).reshape(N_GRP * DEVICE_TOKENS)
        document = jnp.transpose(document, (1, 0, 2)).reshape(N_GRP * DEVICE_TOKENS)
        return group_attention(query_token_rows, paired_token_rows, position, document).reshape(N_GRP, DEVICE_TOKENS, QUERY_HEADS * HEAD_SIZE)
    result = lax.map(one_group, ctx_ids)
    return result.reshape(N_CTX * N_GRP * DEVICE_TOKENS, QUERY_HEADS * HEAD_SIZE)
```

```python
import math

import jax
import jax.numpy as jnp
from jax import lax
from jax.experimental import pallas as pl
from jax.experimental.pallas import tpu as pltpu
from jax.sharding import PartitionSpec as P

QUERY_HEADS = 20
KEY_VALUE_HEADS = 4
HEAD_SIZE = 128
SHARED = QUERY_HEADS // KEY_VALUE_HEADS
X, Z, CORES, G = 4, 8, 2, 8
N_CTX = X * Z * CORES
UNITS = 4
ROWS = N_CTX * UNITS
MESH = pl.DeviceIdType.MESH
F32, BF16 = jnp.float32, jnp.bfloat16
NEGATIVE = -1e30
EXPONENT = math.log2(math.e) / math.sqrt(HEAD_SIZE)
SLOT = {0: 0, 1: 1, 7: 2, 2: 3, 6: 4, 3: 5, 5: 6, 4: 7}
REL = {slot: rel for rel, slot in SLOT.items()}
Q_TILES = QUERY_HEADS // 4


def z_offset(i):
    odd = i % 2
    return odd * ((i + 1) // 2) + (1 - odd) * ((8 - i // 2) % 8)


def kernel(
    slot_ref, doc_ref, q_hbm, kv_hbm, out_hbm,
    q_in, kv_in, send, kv_got, q_got, gathered, q_heads, out_v,
    stage, out_stage, bias_full, bias_a, bias_b,
    in_sem, out_sem, own_sem, send_sem, kv_sem, q_sem, ring_send, ring_recv,
):
    ctx, grp = lax.axis_index("ctx"), lax.axis_index("grp")
    x, z, core = ctx // (Z * CORES), (ctx // CORES) % Z, ctx % CORES
    xk = x * CORES + core

    def peer(n):
        i, w = n // 8, n % 8
        return (((x + w // 2) % X) * Z + (z + z_offset(i)) % Z) * CORES + (core + w % 2) % CORES

    load_kv = pltpu.make_async_copy(kv_hbm, kv_in, in_sem.at[0])
    load_q = pltpu.make_async_copy(q_hbm, q_in, in_sem.at[1])
    load_kv.start()
    load_q.start()

    barrier = pltpu.get_barrier_semaphore()

    def greet(n, carry):
        pl.semaphore_signal(barrier, inc=1, device_id=(peer(n), grp), device_id_type=MESH)
        return carry

    lax.fori_loop(1, N_CTX, greet, 0)
    right, left = (ctx, (grp + 1) % G), (ctx, (grp + G - 1) % G)
    for side in (right, left):
        pl.semaphore_signal(barrier, inc=1, device_id=side, device_id_type=MESH)

    place = lax.broadcasted_iota(jnp.int32, (ROWS, ROWS), 0)
    wanted = (place % N_CTX) * UNITS + place // N_CTX
    permute = jnp.where(slot_ref[...] == wanted, 1.0, 0.0).astype(BF16)

    def lay_out(tile, values):
        part = stage.at[tile % 2]
        for j in range(4):
            for k in range(UNITS):
                part[pl.ds(j * 4 + k, N_CTX, stride=16), :] = values[j][k * N_CTX : (k + 1) * N_CTX]
        send[tile] = part[...].reshape(N_CTX, 16, HEAD_SIZE).astype(BF16)

    def kv_copy(tile, n, place, sem):
        t = peer(n)
        return pltpu.make_async_remote_copy(
            src_ref=send.at[tile, t], dst_ref=kv_got.at[tile, n // 8 * 8 + xk],
            send_sem=send_sem.at[tile], recv_sem=sem, device_id=(t, grp), device_id_type=MESH,
        )

    def send_kv(tile):
        pltpu.make_async_copy(send.at[tile, ctx], kv_got.at[tile, xk], own_sem.at[tile]).start()
        for p in range(4):
            def go(n, carry, p=p):
                kv_copy(tile, n, None, kv_sem.at[tile, p]).start()
                return carry

            lax.fori_loop(max(1, 16 * p), 16 * p + 16, go, 0)

    def send_q(tile):
        pltpu.make_async_copy(send.at[tile + 2, ctx], q_got.at[tile, ctx], own_sem.at[tile + 2]).start()

        def go(n, carry):
            t = peer(n)
            pltpu.make_async_remote_copy(
                src_ref=send.at[tile + 2, t], dst_ref=q_got.at[tile, ctx],
                send_sem=send_sem.at[tile + 2], recv_sem=q_sem.at[tile], device_id=(t, grp), device_id_type=MESH,
            ).start()
            return carry

        lax.fori_loop(1, N_CTX, go, 0)

    def prepare_q(tile):
        y = jnp.dot(permute, q_in[:, tile * 512 : tile * 512 + 512], preferred_element_type=F32)
        lay_out(tile + 2, [y[:, j * 128 : j * 128 + 128] for j in range(4)])
        send_q(tile)

    def prepare_kv(tile):
        k2 = jnp.dot(permute, kv_in[:, tile * 256 : tile * 256 + 256], preferred_element_type=F32)
        v2 = jnp.dot(permute, kv_in[:, 512 + tile * 256 : 512 + tile * 256 + 256], preferred_element_type=F32)
        lay_out(tile, [k2[:, :128], v2[:, :128], k2[:, 128:], v2[:, 128:]])

    def ring(way, pair, p, step):
        rel_from, rel_to = ((-step) % G, (-step - 1) % G) if way == 0 else (step, step + 1)
        return pltpu.make_async_remote_copy(
            src_ref=gathered.at[pair, p, SLOT[rel_from]], dst_ref=gathered.at[pair, p, SLOT[rel_to]],
            send_sem=ring_send.at[way, pair, p, step], recv_sem=ring_recv.at[way, pair, p, step],
            device_id=right if way == 0 else left, device_id_type=MESH,
        )

    def ring_has(way, p, step):
        return step < 3 or (p < 2) == (way == 0)

    def open_ring(pair, p):
        n = 15 if p == 0 else 16
        piece = kv_got.at[pair, pl.ds(0, n)]
        if p == 0:
            own = kv_got.at[pair, 0]
            pltpu.make_async_copy(own, own, own_sem.at[pair]).wait()
        pltpu.make_async_copy(piece, piece, kv_sem.at[pair, p]).wait()
        part = stage.at[p % 2]
        part[0:256, :] = kv_got[pair, 16 * p : 16 * p + 16].reshape(256, HEAD_SIZE).astype(F32)
        for j in range(4):
            for k in range(UNITS):
                gathered[pair, p, 0, j, k] = part[pl.ds(j * 4 + k, 16, stride=16), :].astype(BF16)
        for way in range(2):
            ring(way, pair, p, 0).start()

    def pass_on(pair, p, step):
        for way in range(2):
            ring(way, pair, p, step - 1).wait_recv()
            if ring_has(way, p, step):
                ring(way, pair, p, step).start()

    def last_of_ring(pair, p):
        ring(0 if p < 2 else 1, pair, p, 3).wait_recv()

    def take_q(tile):
        own = q_got.at[tile, 0]
        pltpu.make_async_copy(own, own, own_sem.at[tile + 2]).wait()
        piece = q_got.at[tile, pl.ds(0, N_CTX - 1)]
        pltpu.make_async_copy(piece, piece, q_sem.at[tile]).wait()
        part = stage.at[tile % 2]
        part[...] = q_got[tile].reshape(N_CTX * 16, HEAD_SIZE).astype(F32)
        for j in range(4):
            for k in range(UNITS):
                q_heads[tile * 4 + j, k] = part[pl.ds(j * 4 + k, N_CTX, stride=16), :].astype(BF16)

    def fill_bias(ref, low, high):
        wide = high - low
        width = 64 * wide
        docs = [
            jnp.sum(jnp.where(slot_ref[...] == ctx * UNITS + k, doc_ref[...], 0).astype(F32), axis=1, keepdims=True)
            for k in range(UNITS)
        ]
        at = lax.broadcasted_iota(jnp.int32, (N_CTX, width), 1)
        p, place, source = at // (16 * wide), (at // 16) % wide, at % 16
        rel = jnp.zeros_like(at)
        for s in range(low, high):
            rel = jnp.where(place == s - low, REL[s], rel)
        xk_key, i = source % 8, 2 * p + source // 8
        z_key = (z - z_offset(i) + Z) % Z
        key = ((xk_key // 2 * Z + z_key) * CORES + xk_key % 2) * G + (grp + rel) % G
        query = lax.broadcasted_iota(jnp.int32, (N_CTX, width), 0) * G + grp
        causal = jnp.where(key <= query, 0.0, NEGATIVE)
        for k in range(UNITS):
            for k2 in range(k):
                ref[k, :, k2 * width : (k2 + 1) * width] = jnp.broadcast_to(
                    jnp.where(docs[k2] == docs[k], 0.0, NEGATIVE), (N_CTX, width)
                )
            ref[k, :, k * width : (k + 1) * width] = causal

    def attend(h, stages):
        pair, jk = h // 2, h % 2 * 2
        for k in range(UNITS):
            q = q_heads[h * SHARED : (h + 1) * SHARED, k].reshape(SHARED * N_CTX, HEAD_SIZE)
            top = total = None
            for low, high, bias in stages:
                width = 64 * (high - low)
                count = width * (k + 1)

                def rows(j, low=low, high=high, width=width):
                    return jnp.concatenate(
                        [gathered[pair, :, low:high, j, k2].reshape(width, HEAD_SIZE) for k2 in range(k + 1)], axis=0
                    )

                s = lax.dot_general(q, rows(jk), (((1,), (1,)), ((), ())), preferred_element_type=F32)
                s = s.reshape(SHARED, N_CTX, count) + bias[k, :, 0:count][None]
                s = s.reshape(SHARED * N_CTX, count)
                new_top = jnp.max(s, axis=1, keepdims=True)
                if top is not None:
                    new_top = jnp.maximum(top, new_top)
                weights = jnp.exp2((s - new_top) * EXPONENT).astype(BF16)
                values = jnp.concatenate([rows(jk + 1), jnp.ones((count, HEAD_SIZE), BF16)], axis=1)
                part = jnp.dot(weights, values, preferred_element_type=F32)
                total = part if top is None else total * jnp.exp2((top - new_top) * EXPONENT) + part
                top = new_top
            result = total[:, :HEAD_SIZE] / total[:, HEAD_SIZE:]
            for i in range(SHARED):
                out_stage[i, pl.ds(k, N_CTX, stride=UNITS), :] = result[i * N_CTX : (i + 1) * N_CTX]
        for i in range(SHARED):
            col = (h * SHARED + i) * HEAD_SIZE
            out_v[:, col : col + HEAD_SIZE] = out_stage[i].astype(BF16)
        store(h).start()

    def store(h):
        cols = pl.ds(h * SHARED * HEAD_SIZE, SHARED * HEAD_SIZE)
        return pltpu.make_async_copy(out_v.at[:, cols], out_hbm.at[:, cols], out_sem.at[h])

    load_kv.wait()
    prepare_kv(0)
    pl.semaphore_wait(barrier, N_CTX - 1 + 2)
    send_kv(0)
    prepare_kv(1)
    send_kv(1)
    load_q.wait()
    for tile in range(4):
        prepare_q(tile)
        open_ring(0, tile)
    prepare_q(4)
    fill_bias(bias_full, 0, G)
    fill_bias(bias_a, 0, 4)
    fill_bias(bias_b, 4, G)
    for p in range(4):
        pass_on(0, p, 1)
    for p in range(4):
        pass_on(0, p, 2)
    for p in range(4):
        pass_on(0, p, 3)
        open_ring(1, p)
    for p in range(4):
        last_of_ring(0, p)
    take_q(0)
    take_q(1)
    attend(0, [(0, G, bias_full)])
    for p in range(4):
        pass_on(1, p, 1)
    take_q(2)
    attend(1, [(0, G, bias_full)])
    for p in range(4):
        pass_on(1, p, 2)
    take_q(3)
    for p in range(4):
        pass_on(1, p, 3)
    take_q(4)
    for p in range(4):
        last_of_ring(1, p)
    attend(2, [(0, G, bias_full)])
    attend(3, [(0, G, bias_full)])

    for h in range(KEY_VALUE_HEADS):
        store(h).wait()
    for tile in range(2 + Q_TILES):
        piece = send.at[tile, pl.ds(0, N_CTX - 1)]
        pltpu.make_async_copy(piece, piece, send_sem.at[tile]).wait()
    for way in range(2):
        for pair in range(2):
            for p in range(4):
                for step in range(4):
                    if ring_has(way, p, step):
                        ring(way, pair, p, step).wait_send()


def local(queries, key_value_rows, unit_slot, unit_doc):
    dma = pltpu.SemaphoreType.DMA
    tiles = 2 + Q_TILES
    any_spec = pl.BlockSpec(memory_space=pl.ANY)
    vmem_spec = pl.BlockSpec(memory_space=pltpu.VMEM)
    return pl.pallas_call(
        kernel,
        name="repacked_attention",
        out_shape=jax.ShapeDtypeStruct(queries.shape, BF16),
        in_specs=[vmem_spec, vmem_spec, any_spec, any_spec],
        out_specs=any_spec,
        scratch_shapes=[
            pltpu.VMEM(queries.shape, BF16),
            pltpu.VMEM(key_value_rows.shape, BF16),
            pltpu.VMEM((tiles, N_CTX, 16, HEAD_SIZE), BF16),
            pltpu.VMEM((2, N_CTX, 16, HEAD_SIZE), BF16),
            pltpu.VMEM((Q_TILES, N_CTX, 16, HEAD_SIZE), BF16),
            pltpu.VMEM((2, 4, G, 4, UNITS, 16, HEAD_SIZE), BF16),
            pltpu.VMEM((QUERY_HEADS, UNITS, N_CTX, HEAD_SIZE), BF16),
            pltpu.VMEM(queries.shape, BF16),
            pltpu.VMEM((2, N_CTX * 16, HEAD_SIZE), F32),
            pltpu.VMEM((SHARED, ROWS, HEAD_SIZE), F32),
            pltpu.VMEM((UNITS, N_CTX, 64 * G * UNITS), F32),
            pltpu.VMEM((UNITS, N_CTX, 64 * 4 * UNITS), F32),
            pltpu.VMEM((UNITS, N_CTX, 64 * 4 * UNITS), F32),
            dma((2,)),
            dma((KEY_VALUE_HEADS,)),
            dma((tiles,)),
            dma((tiles,)),
            dma((2, 4)),
            dma((Q_TILES,)),
            dma((2, 2, 4, 4)),
            dma((2, 2, 4, 4)),
        ],
        compiler_params=pltpu.CompilerParams(
            collective_id=0, has_side_effects=True, vmem_limit_bytes=56 * 2**20
        ),
        cost_estimate=pl.CostEstimate(flops=5 * 10**9, bytes_accessed=4 * 10**6, transcendentals=6 * 10**6),
    )(unit_slot.reshape(1, -1), unit_doc.reshape(1, -1), queries, key_value_rows)


def solution(mesh):
    in_specs = (P(("ctx", "grp"), None), P(("ctx", "grp"), None), P(), P())
    out_specs = P(("ctx", "grp"), None)
    return jax.shard_map(local, mesh=mesh, in_specs=in_specs, out_specs=out_specs, check_vma=False)
```

```python
import math

import jax
import jax.numpy as jnp
from jax import lax
from jax.experimental import pallas as pl
from jax.experimental.pallas import tpu as pltpu
from jax.sharding import PartitionSpec as P

QUERY_HEADS = 20
KEY_VALUE_HEADS = 4
HEAD_SIZE = 128
SHARED = QUERY_HEADS // KEY_VALUE_HEADS
X, Z, CORES, G = 4, 8, 2, 8
N_CTX = X * Z * CORES
UNITS = 4
ROWS = N_CTX * UNITS
MESH = pl.DeviceIdType.MESH
F32, BF16 = jnp.float32, jnp.bfloat16
NEGATIVE = -1e30
EXPONENT = math.log2(math.e) / math.sqrt(HEAD_SIZE)
SLOT = {0: 0, 1: 1, 7: 2, 2: 3, 6: 4, 3: 5, 5: 6, 4: 7}
REL = {slot: rel for rel, slot in SLOT.items()}
Q_TILES = QUERY_HEADS // 4
LEAD = 4


def z_offset(i):
    odd = i % 2
    return odd * ((i + 1) // 2) + (1 - odd) * ((8 - i // 2) % 8)


def kernel(
    slot_ref, doc_ref, q_hbm, kv_hbm, out_ref,
    q_in, kv_in, send, kv_got, q_got, gathered, q_heads,
    stage, out_stage, bias_full, bias_a, bias_b, bias_c,
    in_sem, own_sem, send_sem, kv_sem, q_sem, ring_send, ring_recv,
):
    ctx, grp = lax.axis_index("ctx"), lax.axis_index("grp")
    x, z, core = ctx // (Z * CORES), (ctx // CORES) % Z, ctx % CORES
    xk = x * CORES + core

    def peer(n):
        i, w = n // 8, n % 8
        return (((x + w // 2) % X) * Z + (z + z_offset(i)) % Z) * CORES + (core + w % 2) % CORES

    load_kv = pltpu.make_async_copy(kv_hbm, kv_in, in_sem.at[0])
    load_q = pltpu.make_async_copy(q_hbm, q_in, in_sem.at[1])
    load_kv.start()
    load_q.start()

    barrier = pltpu.get_barrier_semaphore()

    def greet(n, carry):
        pl.semaphore_signal(barrier, inc=1, device_id=(peer(n), grp), device_id_type=MESH)
        return carry

    lax.fori_loop(1, N_CTX, greet, 0)
    right, left = (ctx, (grp + 1) % G), (ctx, (grp + G - 1) % G)
    for side in (right, left):
        pl.semaphore_signal(barrier, inc=1, device_id=side, device_id_type=MESH)

    place = lax.broadcasted_iota(jnp.int32, (ROWS, ROWS), 0)
    wanted = (place % N_CTX) * UNITS + place // N_CTX
    permute = jnp.where(slot_ref[...] == wanted, 1.0, 0.0).astype(BF16)

    def lay_out(tile, values):
        part = stage.at[tile % 2]
        for j in range(4):
            for k in range(UNITS):
                part[pl.ds(j * 4 + k, N_CTX, stride=16), :] = values[j][k * N_CTX : (k + 1) * N_CTX]
        send[tile] = part[...].reshape(N_CTX, 16, HEAD_SIZE).astype(BF16)

    def send_kv(tile, p):
        if p == 0:
            pltpu.make_async_copy(send.at[tile, ctx], kv_got.at[tile, xk], own_sem.at[tile]).start()

        def go(n, carry):
            t = peer(n)
            pltpu.make_async_remote_copy(
                src_ref=send.at[tile, t], dst_ref=kv_got.at[tile, n // 8 * 8 + xk],
                send_sem=send_sem.at[tile], recv_sem=kv_sem.at[tile, p], device_id=(t, grp), device_id_type=MESH,
            ).start()
            return carry

        lax.fori_loop(max(1, 16 * p), 16 * p + 16, go, 0)

    def send_q(tile, part):
        if part == 0:
            pltpu.make_async_copy(send.at[tile + 2, ctx], q_got.at[tile, ctx], own_sem.at[tile + 2]).start()

        def go(m, carry):
            t = peer(m // 2 * 8 + part * 2 + m % 2)
            pltpu.make_async_remote_copy(
                src_ref=send.at[tile + 2, t], dst_ref=q_got.at[tile, ctx],
                send_sem=send_sem.at[tile + 2], recv_sem=q_sem.at[tile], device_id=(t, grp), device_id_type=MESH,
            ).start()
            return carry

        lax.fori_loop(1 if part == 0 else 0, 16, go, 0)

    def prepare_q(tile):
        y = jnp.dot(permute, q_in[:, tile * 512 : tile * 512 + 512], preferred_element_type=F32)
        lay_out(tile + 2, [y[:, j * 128 : j * 128 + 128] for j in range(4)])

    def prepare_kv(tile):
        k2 = jnp.dot(permute, kv_in[:, tile * 256 : tile * 256 + 256], preferred_element_type=F32)
        v2 = jnp.dot(permute, kv_in[:, 512 + tile * 256 : 512 + tile * 256 + 256], preferred_element_type=F32)
        lay_out(tile, [k2[:, :128], v2[:, :128], k2[:, 128:], v2[:, 128:]])

    def ring(way, pair, p, step):
        rel_from, rel_to = ((-step) % G, (-step - 1) % G) if way == 0 else (step, step + 1)
        return pltpu.make_async_remote_copy(
            src_ref=gathered.at[pair, p, SLOT[rel_from]], dst_ref=gathered.at[pair, p, SLOT[rel_to]],
            send_sem=ring_send.at[way, pair, p, step], recv_sem=ring_recv.at[way, pair, p, step],
            device_id=right if way == 0 else left, device_id_type=MESH,
        )

    def ring_has(way, p, step):
        return step < 3 or (p < 2) == (way == 0)

    def open_ring(pair, p):
        n = 15 if p == 0 else 16
        piece = kv_got.at[pair, pl.ds(0, n)]
        if p == 0:
            own = kv_got.at[pair, 0]
            pltpu.make_async_copy(own, own, own_sem.at[pair]).wait()
        pltpu.make_async_copy(piece, piece, kv_sem.at[pair, p]).wait()
        part = stage.at[p % 2]
        part[0:256, :] = kv_got[pair, 16 * p : 16 * p + 16].reshape(256, HEAD_SIZE).astype(F32)
        for j in range(4):
            for k in range(UNITS):
                gathered[pair, p, 0, j, k] = part[pl.ds(j * 4 + k, 16, stride=16), :].astype(BF16)
        for way in range(2):
            ring(way, pair, p, 0).start()

    def pass_on(pair, p, step):
        for way in range(2):
            ring(way, pair, p, step - 1).wait_recv()
            if ring_has(way, p, step):
                ring(way, pair, p, step).start()

    def last_of_ring(pair, p):
        ring(0 if p < 2 else 1, pair, p, 3).wait_recv()

    def take_q(tile):
        own = q_got.at[tile, 0]
        pltpu.make_async_copy(own, own, own_sem.at[tile + 2]).wait()
        piece = q_got.at[tile, pl.ds(0, N_CTX - 1)]
        pltpu.make_async_copy(piece, piece, q_sem.at[tile]).wait()
        part = stage.at[tile % 2]
        part[...] = q_got[tile].reshape(N_CTX * 16, HEAD_SIZE).astype(F32)
        for j in range(4):
            for k in range(UNITS):
                q_heads[tile * 4 + j, k] = part[pl.ds(j * 4 + k, N_CTX, stride=16), :].astype(BF16)

    def fill_bias(ref, low, high):
        wide = high - low
        width = 64 * wide
        docs = [
            jnp.sum(jnp.where(slot_ref[...] == ctx * UNITS + k, doc_ref[...], 0).astype(F32), axis=1, keepdims=True)
            for k in range(UNITS)
        ]
        at = lax.broadcasted_iota(jnp.int32, (N_CTX, width), 1)
        p, place, source = at // (16 * wide), (at // 16) % wide, at % 16
        rel = jnp.zeros_like(at)
        for s in range(low, high):
            rel = jnp.where(place == s - low, REL[s], rel)
        xk_key, i = source % 8, 2 * p + source // 8
        z_key = (z - z_offset(i) + Z) % Z
        key = ((xk_key // 2 * Z + z_key) * CORES + xk_key % 2) * G + (grp + rel) % G
        query = lax.broadcasted_iota(jnp.int32, (N_CTX, width), 0) * G + grp
        causal = jnp.where(key <= query, 0.0, NEGATIVE)
        for k in range(UNITS):
            for k2 in range(k):
                ref[k, :, k2 * width : (k2 + 1) * width] = jnp.broadcast_to(
                    jnp.where(docs[k2] == docs[k], 0.0, NEGATIVE), (N_CTX, width)
                )
            ref[k, :, k * width : (k + 1) * width] = causal

    def attend(h, k, low, high, bias, state=None):
        pair, jk = h // 2, h % 2 * 2
        width = 64 * (high - low)
        q = q_heads[h * SHARED : (h + 1) * SHARED, k].reshape(SHARED * N_CTX, HEAD_SIZE)
        group = max(1, 512 // width)
        for last in range(k, -1, -group):
            units = range(max(0, last - group + 1), last + 1)
            count = width * len(units)

            def rows(j):
                return jnp.concatenate([gathered[pair, :, low:high, j, k2].reshape(width, HEAD_SIZE) for k2 in units], axis=0)

            s = lax.dot_general(q, rows(jk), (((1,), (1,)), ((), ())), preferred_element_type=F32)
            s = s.reshape(SHARED, N_CTX, count) + bias[k, :, units[0] * width : units[0] * width + count][None]
            s = s.reshape(SHARED * N_CTX, count)
            top = jnp.max(s, axis=1, keepdims=True)
            if state is not None:
                top = jnp.maximum(top, state[0])
            weights = jnp.exp2((s - top) * EXPONENT).astype(BF16)
            values = jnp.concatenate([rows(jk + 1), jnp.ones((count, HEAD_SIZE), BF16)], axis=1)
            total = jnp.dot(weights, values, preferred_element_type=F32)
            if state is not None:
                total = total + state[1] * jnp.exp2((state[0] - top) * EXPONENT)
            state = top, total
        return state

    def finish(h, k, state):
        total = state[1]
        result = total[:, :HEAD_SIZE] / total[:, HEAD_SIZE:]
        for i in range(SHARED):
            out_stage[i, pl.ds(k, N_CTX, stride=UNITS), :] = result[i * N_CTX : (i + 1) * N_CTX]
        if k == UNITS - 1:
            for i in range(SHARED):
                col = (h * SHARED + i) * HEAD_SIZE
                out_ref[:, col : col + HEAD_SIZE] = out_stage[i].astype(BF16)

    parts = [(tile, p) for tile in range(2 + Q_TILES) for p in range(4)]
    issued = [0]

    def issue(count):
        while issued[0] < min(count, len(parts)):
            tile, p = parts[issued[0]]
            issued[0] += 1
            if tile < 2:
                send_kv(tile, p)
            else:
                if p == 0 and tile >= 4:
                    prepare_q(tile - 2)
                send_q(tile - 2, p)

    def run(events):
        for pair, p, step in events:
            if step == 0:
                open_ring(pair, p)
            elif step < 4:
                pass_on(pair, p, step)
            else:
                last_of_ring(pair, p)
                continue
            issue(issued[0] + 1)

    load_kv.wait()
    prepare_kv(0)
    prepare_kv(1)
    load_q.wait()
    prepare_q(0)
    prepare_q(1)
    pl.semaphore_wait(barrier, N_CTX - 1 + 2)
    issue(LEAD)
    run([(0, 0, 0), (0, 1, 0), (0, 0, 1), (0, 2, 0), (0, 1, 1), (0, 3, 0), (0, 2, 1), (0, 0, 2), (0, 3, 1), (0, 1, 2)])
    run([(1, 0, 0), (0, 2, 2), (0, 0, 3), (0, 3, 2), (0, 1, 3), (1, 1, 0), (1, 2, 0), (0, 2, 3), (0, 3, 3), (1, 3, 0)])
    fill_bias(bias_full, 0, G)
    fill_bias(bias_a, 0, 4)
    fill_bias(bias_b, 4, 6)
    fill_bias(bias_c, 6, G)
    run([(1, 0, 1), (1, 1, 1)])
    run([(0, p, 4) for p in range(4)])
    take_q(0)
    take_q(1)
    finish(0, 0, attend(0, 0, 0, G, bias_full))
    finish(0, 1, attend(0, 1, 0, G, bias_full))
    run([(1, 2, 1)])
    finish(0, 2, attend(0, 2, 0, G, bias_full))
    run([(1, 3, 1)])
    finish(0, 3, attend(0, 3, 0, G, bias_full))
    run([(1, 0, 2), (1, 1, 2)])
    issue(len(parts))
    take_q(2)
    finish(1, 0, attend(1, 0, 0, G, bias_full))
    finish(1, 1, attend(1, 1, 0, G, bias_full))
    run([(1, 2, 2)])
    finish(1, 2, attend(1, 2, 0, G, bias_full))
    run([(1, 3, 2)])
    finish(1, 3, attend(1, 3, 0, G, bias_full))
    run([(1, 0, 3), (1, 2, 3)])
    take_q(3)
    early = {}
    for k in range(UNITS):
        early[2, k] = attend(2, k, 0, 4, bias_a)
    run([(1, 1, 3), (1, 3, 3)])
    for k in range(UNITS):
        early[2, k] = attend(2, k, 4, 6, bias_b, early[2, k])
    take_q(4)
    for k in range(UNITS):
        early[3, k] = attend(3, k, 0, 4, bias_a)
    for k in range(UNITS):
        early[3, k] = attend(3, k, 4, 6, bias_b, early[3, k])
    run([(1, p, 4) for p in range(4)])
    for h in (2, 3):
        for k in range(UNITS):
            finish(h, k, attend(h, k, 6, G, bias_c, early[h, k]))

    for tile in range(2 + Q_TILES):
        piece = send.at[tile, pl.ds(0, N_CTX - 1)]
        pltpu.make_async_copy(piece, piece, send_sem.at[tile]).wait()
    for way in range(2):
        for pair in range(2):
            for p in range(4):
                for step in range(4):
                    if ring_has(way, p, step):
                        ring(way, pair, p, step).wait_send()


def local(queries, key_value_rows, unit_slot, unit_doc):
    dma = pltpu.SemaphoreType.DMA
    tiles = 2 + Q_TILES
    any_spec = pl.BlockSpec(memory_space=pl.ANY)
    vmem_spec = pl.BlockSpec(memory_space=pltpu.VMEM)
    return pl.pallas_call(
        kernel,
        name="repacked_attention",
        out_shape=pltpu.VMEM(queries.shape, BF16),
        in_specs=[vmem_spec, vmem_spec, any_spec, any_spec],
        out_specs=vmem_spec,
        scratch_shapes=[
            pltpu.VMEM(queries.shape, BF16),
            pltpu.VMEM(key_value_rows.shape, BF16),
            pltpu.VMEM((tiles, N_CTX, 16, HEAD_SIZE), BF16),
            pltpu.VMEM((2, N_CTX, 16, HEAD_SIZE), BF16),
            pltpu.VMEM((Q_TILES, N_CTX, 16, HEAD_SIZE), BF16),
            pltpu.VMEM((2, 4, G, 4, UNITS, 16, HEAD_SIZE), BF16),
            pltpu.VMEM((QUERY_HEADS, UNITS, N_CTX, HEAD_SIZE), BF16),
            pltpu.VMEM((2, N_CTX * 16, HEAD_SIZE), F32),
            pltpu.VMEM((SHARED, ROWS, HEAD_SIZE), F32),
            pltpu.VMEM((UNITS, N_CTX, 64 * G * UNITS), F32),
            pltpu.VMEM((UNITS, N_CTX, 64 * 4 * UNITS), F32),
            pltpu.VMEM((UNITS, N_CTX, 64 * 2 * UNITS), F32),
            pltpu.VMEM((UNITS, N_CTX, 64 * 2 * UNITS), F32),
            dma((2,)),
            dma((tiles,)),
            dma((tiles,)),
            dma((2, 4)),
            dma((Q_TILES,)),
            dma((2, 2, 4, 4)),
            dma((2, 2, 4, 4)),
        ],
        compiler_params=pltpu.CompilerParams(
            collective_id=0, has_side_effects=True, vmem_limit_bytes=56 * 2**20
        ),
        cost_estimate=pl.CostEstimate(flops=5 * 10**9, bytes_accessed=4 * 10**6, transcendentals=6 * 10**6),
    )(unit_slot.reshape(1, -1), unit_doc.reshape(1, -1), queries, key_value_rows)


def solution(mesh):
    in_specs = (P(("ctx", "grp"), None), P(("ctx", "grp"), None), P(), P())
    out_specs = P(("ctx", "grp"), None)
    return jax.shard_map(local, mesh=mesh, in_specs=in_specs, out_specs=out_specs, check_vma=False)
```

```python
import math

import jax
import jax.numpy as jnp
from jax import lax
from jax.experimental import pallas as pl
from jax.experimental.pallas import tpu as pltpu
from jax.sharding import PartitionSpec as P

QUERY_HEADS = 20
KEY_VALUE_HEADS = 4
HEAD_SIZE = 128
SHARED = QUERY_HEADS // KEY_VALUE_HEADS
X, Z, CORES, G = 4, 8, 2, 8
N_CTX = X * Z * CORES
UNITS = 4
ROWS = N_CTX * UNITS
MESH = pl.DeviceIdType.MESH
F32, BF16 = jnp.float32, jnp.bfloat16
NEGATIVE = -1e30
EXPONENT = math.log2(math.e) / math.sqrt(HEAD_SIZE)
SLOT = {0: 0, 1: 1, 7: 2, 2: 3, 6: 4, 3: 5, 5: 6, 4: 7}
REL = {slot: rel for rel, slot in SLOT.items()}
Q_TILES = QUERY_HEADS // 4
LEAD = 5


def z_offset(i):
    odd = i % 2
    return odd * ((i + 1) // 2) + (1 - odd) * ((8 - i // 2) % 8)


def kernel(
    slot_ref, doc_ref, q_hbm, kv_hbm, out_ref,
    q_in, kv_in, send, kv_got, q_got, gathered, q_heads,
    stage, out_stage, bias_a, bias_b, bias_c,
    in_sem, own_sem, send_sem, kv_sem, q_sem, ring_send, ring_recv,
):
    ctx, grp = lax.axis_index("ctx"), lax.axis_index("grp")
    x, z, core = ctx // (Z * CORES), (ctx // CORES) % Z, ctx % CORES
    xk = x * CORES + core

    def peer(n):
        i, w = n // 8, n % 8
        return (((x + w // 2) % X) * Z + (z + z_offset(i)) % Z) * CORES + (core + w % 2) % CORES

    load_kv = pltpu.make_async_copy(kv_hbm, kv_in, in_sem.at[0])
    load_q = pltpu.make_async_copy(q_hbm, q_in, in_sem.at[1])
    load_kv.start()
    load_q.start()

    barrier = pltpu.get_barrier_semaphore()

    def greet(n, carry):
        pl.semaphore_signal(barrier, inc=1, device_id=(peer(n), grp), device_id_type=MESH)
        return carry

    lax.fori_loop(1, N_CTX, greet, 0)
    right, left = (ctx, (grp + 1) % G), (ctx, (grp + G - 1) % G)
    for side in (right, left):
        pl.semaphore_signal(barrier, inc=1, device_id=side, device_id_type=MESH)

    place = lax.broadcasted_iota(jnp.int32, (ROWS, ROWS), 0)
    wanted = (place % N_CTX) * UNITS + place // N_CTX
    permute = jnp.where(slot_ref[...] == wanted, 1.0, 0.0).astype(BF16)

    def lay_out(tile, values):
        part = stage.at[tile % 2]
        for j in range(4):
            for k in range(UNITS):
                part[pl.ds(j * 4 + k, N_CTX, stride=16), :] = values[j][k * N_CTX : (k + 1) * N_CTX]
        send[tile] = part[...].reshape(N_CTX, 16, HEAD_SIZE).astype(BF16)

    def send_kv(tile, p):
        if p == 0:
            pltpu.make_async_copy(send.at[tile, ctx], kv_got.at[tile, xk], own_sem.at[tile]).start()

        def go(n, carry):
            t = peer(n)
            pltpu.make_async_remote_copy(
                src_ref=send.at[tile, t], dst_ref=kv_got.at[tile, n // 8 * 8 + xk],
                send_sem=send_sem.at[tile], recv_sem=kv_sem.at[tile, p], device_id=(t, grp), device_id_type=MESH,
            ).start()
            return carry

        lax.fori_loop(max(1, 16 * p), 16 * p + 16, go, 0)

    def send_q(tile, part):
        if part == 0:
            pltpu.make_async_copy(send.at[tile + 2, ctx], q_got.at[tile, ctx], own_sem.at[tile + 2]).start()

        def go(m, carry):
            t = peer(m // 2 * 8 + part * 2 + m % 2)
            pltpu.make_async_remote_copy(
                src_ref=send.at[tile + 2, t], dst_ref=q_got.at[tile, ctx],
                send_sem=send_sem.at[tile + 2], recv_sem=q_sem.at[tile], device_id=(t, grp), device_id_type=MESH,
            ).start()
            return carry

        lax.fori_loop(1 if part == 0 else 0, 16, go, 0)

    def prepare_q(tile):
        y = jnp.dot(permute, q_in[:, tile * 512 : tile * 512 + 512], preferred_element_type=F32)
        lay_out(tile + 2, [y[:, j * 128 : j * 128 + 128] for j in range(4)])

    def prepare_kv(tile):
        k2 = jnp.dot(permute, kv_in[:, tile * 256 : tile * 256 + 256], preferred_element_type=F32)
        v2 = jnp.dot(permute, kv_in[:, 512 + tile * 256 : 512 + tile * 256 + 256], preferred_element_type=F32)
        lay_out(tile, [k2[:, :128], v2[:, :128], k2[:, 128:], v2[:, 128:]])

    def ring(way, pair, p, step):
        rel_from, rel_to = ((-step) % G, (-step - 1) % G) if way == 0 else (step, step + 1)
        return pltpu.make_async_remote_copy(
            src_ref=gathered.at[pair, p, SLOT[rel_from]], dst_ref=gathered.at[pair, p, SLOT[rel_to]],
            send_sem=ring_send.at[way, pair, p, step], recv_sem=ring_recv.at[way, pair, p, step],
            device_id=right if way == 0 else left, device_id_type=MESH,
        )

    def ring_has(way, p, step):
        return step < 3 or (p < 2) == (way == 0)

    def open_ring(pair, p):
        n = 15 if p == 0 else 16
        piece = kv_got.at[pair, pl.ds(0, n)]
        if p == 0:
            own = kv_got.at[pair, 0]
            pltpu.make_async_copy(own, own, own_sem.at[pair]).wait()
        pltpu.make_async_copy(piece, piece, kv_sem.at[pair, p]).wait()
        part = stage.at[p % 2]
        part[0:256, :] = kv_got[pair, 16 * p : 16 * p + 16].reshape(256, HEAD_SIZE).astype(F32)
        for j in range(4):
            for k in range(UNITS):
                gathered[pair, p, 0, j, k] = part[pl.ds(j * 4 + k, 16, stride=16), :].astype(BF16)
        for way in range(2):
            ring(way, pair, p, 0).start()

    def pass_on(pair, p, step):
        for way in range(2):
            ring(way, pair, p, step - 1).wait_recv()
            if ring_has(way, p, step):
                ring(way, pair, p, step).start()

    def last_of_ring(pair, p):
        ring(0 if p < 2 else 1, pair, p, 3).wait_recv()

    def take_q(tile):
        own = q_got.at[tile, 0]
        pltpu.make_async_copy(own, own, own_sem.at[tile + 2]).wait()
        piece = q_got.at[tile, pl.ds(0, N_CTX - 1)]
        pltpu.make_async_copy(piece, piece, q_sem.at[tile]).wait()
        part = stage.at[tile % 2]
        part[...] = q_got[tile].reshape(N_CTX * 16, HEAD_SIZE).astype(F32)
        for j in range(4):
            for k in range(UNITS):
                q_heads[tile * 4 + j, k] = part[pl.ds(j * 4 + k, N_CTX, stride=16), :].astype(BF16)

    def fill_bias(ref, low, high):
        wide = high - low
        width = 64 * wide
        docs = [
            jnp.sum(jnp.where(slot_ref[...] == ctx * UNITS + k, doc_ref[...], 0).astype(F32), axis=1, keepdims=True)
            for k in range(UNITS)
        ]
        at = lax.broadcasted_iota(jnp.int32, (N_CTX, width), 1)
        p, place, source = at // (16 * wide), (at // 16) % wide, at % 16
        rel = jnp.zeros_like(at)
        for s in range(low, high):
            rel = jnp.where(place == s - low, REL[s], rel)
        xk_key, i = source % 8, 2 * p + source // 8
        z_key = (z - z_offset(i) + Z) % Z
        key = ((xk_key // 2 * Z + z_key) * CORES + xk_key % 2) * G + (grp + rel) % G
        query = lax.broadcasted_iota(jnp.int32, (N_CTX, width), 0) * G + grp
        causal = jnp.where(key <= query, 0.0, NEGATIVE)
        for k in range(UNITS):
            for k2 in range(k):
                ref[k, :, k2 * width : (k2 + 1) * width] = jnp.broadcast_to(
                    jnp.where(docs[k2] == docs[k], 0.0, NEGATIVE), (N_CTX, width)
                )
            ref[k, :, k * width : (k + 1) * width] = causal

    def attend(h, k, low, high, bias, state=None):
        pair, jk = h // 2, h % 2 * 2
        width = 64 * (high - low)
        q = q_heads[h * SHARED : (h + 1) * SHARED, k].reshape(SHARED * N_CTX, HEAD_SIZE)
        group = max(1, 512 // width)
        for last in range(k, -1, -group):
            units = range(max(0, last - group + 1), last + 1)
            count = width * len(units)

            def rows(j):
                return jnp.concatenate([gathered[pair, :, low:high, j, k2].reshape(width, HEAD_SIZE) for k2 in units], axis=0)

            s = lax.dot_general(q, rows(jk), (((1,), (1,)), ((), ())), preferred_element_type=F32)
            s = s.reshape(SHARED, N_CTX, count) + bias[k, :, units[0] * width : units[0] * width + count][None]
            s = s.reshape(SHARED * N_CTX, count)
            top = jnp.max(s, axis=1, keepdims=True)
            if state is not None:
                top = jnp.maximum(top, state[0])
            weights = jnp.exp2((s - top) * EXPONENT).astype(BF16)
            values = jnp.concatenate([rows(jk + 1), jnp.ones((count, HEAD_SIZE), BF16)], axis=1)
            total = jnp.dot(weights, values, preferred_element_type=F32)
            if state is not None:
                total = total + state[1] * jnp.exp2((state[0] - top) * EXPONENT)
            state = top, total
        return state

    def finish(h, k, state):
        total = state[1]
        result = total[:, :HEAD_SIZE] / total[:, HEAD_SIZE:]
        for i in range(SHARED):
            out_stage[i, pl.ds(k, N_CTX, stride=UNITS), :] = result[i * N_CTX : (i + 1) * N_CTX]
        if k == UNITS - 1:
            for i in range(SHARED):
                col = (h * SHARED + i) * HEAD_SIZE
                out_ref[:, col : col + HEAD_SIZE] = out_stage[i].astype(BF16)

    parts = [(tile, p) for tile in range(2 + Q_TILES) for p in range(4)]
    issued = [0]

    def issue(count):
        while issued[0] < min(count, len(parts)):
            tile, p = parts[issued[0]]
            issued[0] += 1
            if tile < 2:
                send_kv(tile, p)
            else:
                if p == 0 and tile >= 4:
                    prepare_q(tile - 2)
                send_q(tile - 2, p)

    def run(events):
        for pair, p, step in events:
            if step == 0:
                open_ring(pair, p)
            elif step < 4:
                pass_on(pair, p, step)
            else:
                last_of_ring(pair, p)
                continue
            issue(issued[0] + 1)

    load_kv.wait()
    prepare_kv(0)
    prepare_kv(1)
    load_q.wait()
    prepare_q(0)
    prepare_q(1)
    pl.semaphore_wait(barrier, N_CTX - 1 + 2)
    issue(LEAD)
    state = {}

    def stage_of(h, low, high, bias):
        for k in range(UNITS):
            state[h, k] = attend(h, k, low, high, bias, state.get((h, k)))
            if high == G:
                finish(h, k, state[h, k])

    run([(0, 0, 0), (0, 1, 0), (0, 2, 0), (0, 0, 1), (0, 3, 0), (0, 1, 1), (1, 0, 0), (1, 1, 0), (0, 2, 1), (1, 2, 0)])
    fill_bias(bias_a, 0, 4)
    run([(0, 3, 1), (1, 3, 0)])
    fill_bias(bias_b, 4, 6)
    fill_bias(bias_c, 6, G)
    run([(1, 0, 1), (0, 0, 2), (1, 1, 1), (0, 1, 2), (1, 2, 1), (0, 2, 2)])
    take_q(0)
    run([(1, 3, 1), (0, 3, 2)])
    take_q(1)
    stage_of(0, 0, 4, bias_a)
    run([(1, 0, 2), (0, 0, 3), (1, 1, 2), (0, 1, 3)])
    take_q(2)
    stage_of(1, 0, 4, bias_a)
    run([(1, 2, 2), (0, 2, 3), (1, 3, 2), (0, 3, 3)])
    stage_of(0, 4, 6, bias_b)
    stage_of(1, 4, 6, bias_b)
    run([(1, 0, 3), (1, 1, 3)])
    issue(len(parts))
    take_q(3)
    stage_of(2, 0, 4, bias_a)
    run([(1, 2, 3), (1, 3, 3)])
    stage_of(2, 4, 6, bias_b)
    run([(0, p, 4) for p in range(4)])
    stage_of(0, 6, G, bias_c)
    stage_of(1, 6, G, bias_c)
    take_q(4)
    stage_of(3, 0, 4, bias_a)
    stage_of(3, 4, 6, bias_b)
    run([(1, p, 4) for p in range(4)])
    stage_of(2, 6, G, bias_c)
    stage_of(3, 6, G, bias_c)

    for tile in range(2 + Q_TILES):
        piece = send.at[tile, pl.ds(0, N_CTX - 1)]
        pltpu.make_async_copy(piece, piece, send_sem.at[tile]).wait()
    for way in range(2):
        for pair in range(2):
            for p in range(4):
                for step in range(4):
                    if ring_has(way, p, step):
                        ring(way, pair, p, step).wait_send()


def local(queries, key_value_rows, unit_slot, unit_doc):
    dma = pltpu.SemaphoreType.DMA
    tiles = 2 + Q_TILES
    any_spec = pl.BlockSpec(memory_space=pl.ANY)
    vmem_spec = pl.BlockSpec(memory_space=pltpu.VMEM)
    return pl.pallas_call(
        kernel,
        name="repacked_attention",
        out_shape=pltpu.VMEM(queries.shape, BF16),
        in_specs=[vmem_spec, vmem_spec, any_spec, any_spec],
        out_specs=vmem_spec,
        scratch_shapes=[
            pltpu.VMEM(queries.shape, BF16),
            pltpu.VMEM(key_value_rows.shape, BF16),
            pltpu.VMEM((tiles, N_CTX, 16, HEAD_SIZE), BF16),
            pltpu.VMEM((2, N_CTX, 16, HEAD_SIZE), BF16),
            pltpu.VMEM((Q_TILES, N_CTX, 16, HEAD_SIZE), BF16),
            pltpu.VMEM((2, 4, G, 4, UNITS, 16, HEAD_SIZE), BF16),
            pltpu.VMEM((QUERY_HEADS, UNITS, N_CTX, HEAD_SIZE), BF16),
            pltpu.VMEM((2, N_CTX * 16, HEAD_SIZE), F32),
            pltpu.VMEM((SHARED, ROWS, HEAD_SIZE), F32),
            pltpu.VMEM((UNITS, N_CTX, 64 * 4 * UNITS), F32),
            pltpu.VMEM((UNITS, N_CTX, 64 * 2 * UNITS), F32),
            pltpu.VMEM((UNITS, N_CTX, 64 * 2 * UNITS), F32),
            dma((2,)),
            dma((tiles,)),
            dma((tiles,)),
            dma((2, 4)),
            dma((Q_TILES,)),
            dma((2, 2, 4, 4)),
            dma((2, 2, 4, 4)),
        ],
        compiler_params=pltpu.CompilerParams(
            collective_id=0, has_side_effects=True, vmem_limit_bytes=56 * 2**20
        ),
        cost_estimate=pl.CostEstimate(flops=5 * 10**9, bytes_accessed=4 * 10**6, transcendentals=6 * 10**6),
    )(unit_slot.reshape(1, -1), unit_doc.reshape(1, -1), queries, key_value_rows)


def solution(mesh):
    in_specs = (P(("ctx", "grp"), None), P(("ctx", "grp"), None), P(), P())
    out_specs = P(("ctx", "grp"), None)
    return jax.shard_map(local, mesh=mesh, in_specs=in_specs, out_specs=out_specs, check_vma=False)
```

```python
import math

import jax
import jax.numpy as jnp
from jax import lax
from jax.experimental import pallas as pl
from jax.experimental.pallas import tpu as pltpu
from jax.sharding import PartitionSpec as P

QUERY_HEADS = 20
KEY_VALUE_HEADS = 4
HEAD_SIZE = 128
SHARED = QUERY_HEADS // KEY_VALUE_HEADS
X, Z, CORES, G = 4, 8, 2, 8
N_CTX = X * Z * CORES
UNITS = 4
ROWS = N_CTX * UNITS
MESH = pl.DeviceIdType.MESH
F32, BF16 = jnp.float32, jnp.bfloat16
NEGATIVE = -1e30
EXPONENT = math.log2(math.e) / math.sqrt(HEAD_SIZE)
SLOT = {0: 0, 1: 1, 7: 2, 2: 3, 6: 4, 3: 5, 5: 6, 4: 7}
REL = {slot: rel for rel, slot in SLOT.items()}
Q_TILES = QUERY_HEADS // 4
LEAD = 4


def z_offset(i):
    odd = i % 2
    return odd * ((i + 1) // 2) + (1 - odd) * ((8 - i // 2) % 8)


def kernel(
    slot_ref, doc_ref, q_hbm, kv_hbm, out_ref,
    q_in, kv_in, send, kv_got, q_got, gathered, q_heads,
    stage, out_stage, bias_full, bias_a, bias_b, bias_c,
    in_sem, own_sem, send_sem, kv_sem, q_sem, ring_send, ring_recv,
):
    ctx, grp = lax.axis_index("ctx"), lax.axis_index("grp")
    x, z, core = ctx // (Z * CORES), (ctx // CORES) % Z, ctx % CORES
    xk = x * CORES + core

    def peer(n):
        i, w = n // 8, n % 8
        return (((x + w // 2) % X) * Z + (z + z_offset(i)) % Z) * CORES + (core + w % 2) % CORES

    load_kv = pltpu.make_async_copy(kv_hbm, kv_in, in_sem.at[0])
    load_q = pltpu.make_async_copy(q_hbm, q_in, in_sem.at[1])
    load_kv.start()

    barrier = pltpu.get_barrier_semaphore()

    def greet(n, carry):
        pl.semaphore_signal(barrier, inc=1, device_id=(peer(n), grp), device_id_type=MESH)
        return carry

    lax.fori_loop(1, N_CTX, greet, 0)
    right, left = (ctx, (grp + 1) % G), (ctx, (grp + G - 1) % G)
    for side in (right, left):
        pl.semaphore_signal(barrier, inc=1, device_id=side, device_id_type=MESH)

    place = lax.broadcasted_iota(jnp.int32, (ROWS, ROWS), 0)
    wanted = (place % N_CTX) * UNITS + place // N_CTX
    permute = jnp.where(slot_ref[...] == wanted, 1.0, 0.0).astype(BF16)

    def lay_out(tile, values):
        part = stage.at[tile % 2]
        for j in range(4):
            for k in range(UNITS):
                part[pl.ds(j * 4 + k, N_CTX, stride=16), :] = values[j][k * N_CTX : (k + 1) * N_CTX]
        send[tile] = part[...].reshape(N_CTX, 16, HEAD_SIZE).astype(BF16)

    def send_kv(tile, p):
        if p == 0:
            pltpu.make_async_copy(send.at[tile, ctx], kv_got.at[tile, xk], own_sem.at[tile]).start()

        def go(n, carry):
            t = peer(n)
            pltpu.make_async_remote_copy(
                src_ref=send.at[tile, t], dst_ref=kv_got.at[tile, n // 8 * 8 + xk],
                send_sem=send_sem.at[tile], recv_sem=kv_sem.at[tile, p], device_id=(t, grp), device_id_type=MESH,
            ).start()
            return carry

        lax.fori_loop(max(1, 16 * p), 16 * p + 16, go, 0)

    def send_q(tile, part):
        if part == 0:
            pltpu.make_async_copy(send.at[tile + 2, ctx], q_got.at[tile, ctx], own_sem.at[tile + 2]).start()

        def go(m, carry):
            t = peer(m // 2 * 8 + part * 2 + m % 2)
            pltpu.make_async_remote_copy(
                src_ref=send.at[tile + 2, t], dst_ref=q_got.at[tile, ctx],
                send_sem=send_sem.at[tile + 2], recv_sem=q_sem.at[tile], device_id=(t, grp), device_id_type=MESH,
            ).start()
            return carry

        lax.fori_loop(1 if part == 0 else 0, 16, go, 0)

    def prepare_q(tile):
        y = jnp.dot(permute, q_in[:, tile * 512 : tile * 512 + 512], preferred_element_type=F32)
        lay_out(tile + 2, [y[:, j * 128 : j * 128 + 128] for j in range(4)])

    def prepare_kv(tile):
        k2 = jnp.dot(permute, kv_in[:, tile * 256 : tile * 256 + 256], preferred_element_type=F32)
        v2 = jnp.dot(permute, kv_in[:, 512 + tile * 256 : 512 + tile * 256 + 256], preferred_element_type=F32)
        lay_out(tile, [k2[:, :128], v2[:, :128], k2[:, 128:], v2[:, 128:]])

    def ring(way, pair, p, step):
        rel_from, rel_to = ((-step) % G, (-step - 1) % G) if way == 0 else (step, step + 1)
        return pltpu.make_async_remote_copy(
            src_ref=gathered.at[pair, p, SLOT[rel_from]], dst_ref=gathered.at[pair, p, SLOT[rel_to]],
            send_sem=ring_send.at[way, pair, p, step], recv_sem=ring_recv.at[way, pair, p, step],
            device_id=right if way == 0 else left, device_id_type=MESH,
        )

    def ring_has(way, p, step):
        return step < 3 or (p < 2) == (way == 0)

    def open_ring(pair, p):
        n = 15 if p == 0 else 16
        piece = kv_got.at[pair, pl.ds(0, n)]
        if p == 0:
            own = kv_got.at[pair, 0]
            pltpu.make_async_copy(own, own, own_sem.at[pair]).wait()
        pltpu.make_async_copy(piece, piece, kv_sem.at[pair, p]).wait()
        part = stage.at[p % 2]
        part[0:256, :] = kv_got[pair, 16 * p : 16 * p + 16].reshape(256, HEAD_SIZE).astype(F32)
        for j in range(4):
            for k in range(UNITS):
                gathered[pair, p, 0, j, k] = part[pl.ds(j * 4 + k, 16, stride=16), :].astype(BF16)
        for way in range(2):
            ring(way, pair, p, 0).start()

    def pass_on(pair, p, step):
        for way in range(2):
            ring(way, pair, p, step - 1).wait_recv()
            if ring_has(way, p, step):
                ring(way, pair, p, step).start()

    def last_of_ring(pair, p):
        ring(0 if p < 2 else 1, pair, p, 3).wait_recv()

    def take_q(tile):
        own = q_got.at[tile, 0]
        pltpu.make_async_copy(own, own, own_sem.at[tile + 2]).wait()
        piece = q_got.at[tile, pl.ds(0, N_CTX - 1)]
        pltpu.make_async_copy(piece, piece, q_sem.at[tile]).wait()
        part = stage.at[tile % 2]
        part[...] = q_got[tile].reshape(N_CTX * 16, HEAD_SIZE).astype(F32)
        for j in range(4):
            for k in range(UNITS):
                q_heads[tile * 4 + j, k] = part[pl.ds(j * 4 + k, N_CTX, stride=16), :].astype(BF16)

    def fill_bias(ref, low, high):
        wide = high - low
        width = 64 * wide
        docs = [
            jnp.sum(jnp.where(slot_ref[...] == ctx * UNITS + k, doc_ref[...], 0).astype(F32), axis=1, keepdims=True)
            for k in range(UNITS)
        ]
        at = lax.broadcasted_iota(jnp.int32, (N_CTX, width), 1)
        p, place, source = at // (16 * wide), (at // 16) % wide, at % 16
        rel = jnp.zeros_like(at)
        for s in range(low, high):
            rel = jnp.where(place == s - low, REL[s], rel)
        xk_key, i = source % 8, 2 * p + source // 8
        z_key = (z - z_offset(i) + Z) % Z
        key = ((xk_key // 2 * Z + z_key) * CORES + xk_key % 2) * G + (grp + rel) % G
        query = lax.broadcasted_iota(jnp.int32, (N_CTX, width), 0) * G + grp
        causal = jnp.where(key <= query, 0.0, NEGATIVE)
        for k in range(UNITS):
            for k2 in range(k):
                ref[k, :, k2 * width : (k2 + 1) * width] = jnp.broadcast_to(
                    jnp.where(docs[k2] == docs[k], 0.0, NEGATIVE), (N_CTX, width)
                )
            ref[k, :, k * width : (k + 1) * width] = causal

    def attend(h, k, low, high, bias, state=None):
        pair, jk = h // 2, h % 2 * 2
        width = 64 * (high - low)
        q = q_heads[h * SHARED : (h + 1) * SHARED, k].reshape(SHARED * N_CTX, HEAD_SIZE)
        group = max(1, 512 // width)
        for last in range(k, -1, -group):
            units = range(max(0, last - group + 1), last + 1)
            count = width * len(units)

            def rows(j):
                return jnp.concatenate([gathered[pair, :, low:high, j, k2].reshape(width, HEAD_SIZE) for k2 in units], axis=0)

            s = lax.dot_general(q, rows(jk), (((1,), (1,)), ((), ())), preferred_element_type=F32)
            s = s.reshape(SHARED, N_CTX, count) + bias[k, :, units[0] * width : units[0] * width + count][None]
            s = s.reshape(SHARED * N_CTX, count)
            top = jnp.max(s, axis=1, keepdims=True)
            if state is not None:
                top = jnp.maximum(top, state[0])
            weights = jnp.exp2((s - top) * EXPONENT).astype(BF16)
            values = jnp.concatenate([rows(jk + 1), jnp.ones((count, HEAD_SIZE), BF16)], axis=1)
            total = jnp.dot(weights, values, preferred_element_type=F32)
            if state is not None:
                total = total + state[1] * jnp.exp2((state[0] - top) * EXPONENT)
            state = top, total
        return state

    def finish(h, k, state):
        total = state[1]
        result = total[:, :HEAD_SIZE] / total[:, HEAD_SIZE:]
        for i in range(SHARED):
            out_stage[i, pl.ds(k, N_CTX, stride=UNITS), :] = result[i * N_CTX : (i + 1) * N_CTX]
        if k == UNITS - 1:
            for i in range(SHARED):
                col = (h * SHARED + i) * HEAD_SIZE
                out_ref[:, col : col + HEAD_SIZE] = out_stage[i].astype(BF16)

    parts = [(tile, p) for tile in range(2 + Q_TILES) for p in range(4)]
    issued = [0]

    def issue(count):
        while issued[0] < min(count, len(parts)):
            tile, p = parts[issued[0]]
            issued[0] += 1
            if tile < 2:
                send_kv(tile, p)
            else:
                if p == 0 and tile >= 3:
                    prepare_q(tile - 2)
                send_q(tile - 2, p)

    def run(events):
        for pair, p, step in events:
            if step == 0:
                open_ring(pair, p)
            elif step < 4:
                pass_on(pair, p, step)
            else:
                last_of_ring(pair, p)
                continue
            issue(issued[0] + 1)

    load_kv.wait()
    load_q.start()
    prepare_kv(0)
    pl.semaphore_wait(barrier, N_CTX - 1 + 2)
    issue(4)
    prepare_kv(1)
    issue(LEAD)
    load_q.wait()
    prepare_q(0)
    run([(0, 0, 0), (0, 1, 0), (0, 0, 1), (0, 2, 0), (0, 1, 1), (0, 3, 0), (0, 2, 1), (0, 0, 2), (0, 3, 1), (0, 1, 2)])
    run([(1, 0, 0), (0, 2, 2), (0, 0, 3), (0, 3, 2), (0, 1, 3), (1, 1, 0), (1, 2, 0), (0, 2, 3), (0, 3, 3), (1, 3, 0)])
    fill_bias(bias_full, 0, G)
    fill_bias(bias_a, 0, 4)
    fill_bias(bias_b, 4, 6)
    fill_bias(bias_c, 6, G)
    run([(1, 0, 1), (1, 1, 1)])
    run([(0, p, 4) for p in range(4)])
    take_q(0)
    take_q(1)
    finish(0, 0, attend(0, 0, 0, G, bias_full))
    finish(0, 1, attend(0, 1, 0, G, bias_full))
    run([(1, 2, 1)])
    finish(0, 2, attend(0, 2, 0, G, bias_full))
    run([(1, 3, 1)])
    finish(0, 3, attend(0, 3, 0, G, bias_full))
    run([(1, 0, 2), (1, 1, 2)])
    issue(len(parts))
    take_q(2)
    finish(1, 0, attend(1, 0, 0, G, bias_full))
    finish(1, 1, attend(1, 1, 0, G, bias_full))
    run([(1, 2, 2)])
    finish(1, 2, attend(1, 2, 0, G, bias_full))
    run([(1, 3, 2)])
    finish(1, 3, attend(1, 3, 0, G, bias_full))
    run([(1, 0, 3), (1, 2, 3)])
    take_q(3)
    early = {}
    for k in range(UNITS):
        early[2, k] = attend(2, k, 0, 4, bias_a)
    run([(1, 1, 3), (1, 3, 3)])
    for k in range(UNITS):
        early[2, k] = attend(2, k, 4, 6, bias_b, early[2, k])
    take_q(4)
    for k in range(UNITS):
        early[3, k] = attend(3, k, 0, 4, bias_a)
    for k in range(UNITS):
        early[3, k] = attend(3, k, 4, 6, bias_b, early[3, k])
    run([(1, p, 4) for p in range(4)])
    for h in (2, 3):
        for k in range(UNITS):
            finish(h, k, attend(h, k, 6, G, bias_c, early[h, k]))

    for tile in range(2 + Q_TILES):
        piece = send.at[tile, pl.ds(0, N_CTX - 1)]
        pltpu.make_async_copy(piece, piece, send_sem.at[tile]).wait()
    for way in range(2):
        for pair in range(2):
            for p in range(4):
                for step in range(4):
                    if ring_has(way, p, step):
                        ring(way, pair, p, step).wait_send()


def local(queries, key_value_rows, unit_slot, unit_doc):
    dma = pltpu.SemaphoreType.DMA
    tiles = 2 + Q_TILES
    any_spec = pl.BlockSpec(memory_space=pl.ANY)
    vmem_spec = pl.BlockSpec(memory_space=pltpu.VMEM)
    return pl.pallas_call(
        kernel,
        name="repacked_attention",
        out_shape=pltpu.VMEM(queries.shape, BF16),
        in_specs=[vmem_spec, vmem_spec, any_spec, any_spec],
        out_specs=vmem_spec,
        scratch_shapes=[
            pltpu.VMEM(queries.shape, BF16),
            pltpu.VMEM(key_value_rows.shape, BF16),
            pltpu.VMEM((tiles, N_CTX, 16, HEAD_SIZE), BF16),
            pltpu.VMEM((2, N_CTX, 16, HEAD_SIZE), BF16),
            pltpu.VMEM((Q_TILES, N_CTX, 16, HEAD_SIZE), BF16),
            pltpu.VMEM((2, 4, G, 4, UNITS, 16, HEAD_SIZE), BF16),
            pltpu.VMEM((QUERY_HEADS, UNITS, N_CTX, HEAD_SIZE), BF16),
            pltpu.VMEM((2, N_CTX * 16, HEAD_SIZE), F32),
            pltpu.VMEM((SHARED, ROWS, HEAD_SIZE), F32),
            pltpu.VMEM((UNITS, N_CTX, 64 * G * UNITS), F32),
            pltpu.VMEM((UNITS, N_CTX, 64 * 4 * UNITS), F32),
            pltpu.VMEM((UNITS, N_CTX, 64 * 2 * UNITS), F32),
            pltpu.VMEM((UNITS, N_CTX, 64 * 2 * UNITS), F32),
            dma((2,)),
            dma((tiles,)),
            dma((tiles,)),
            dma((2, 4)),
            dma((Q_TILES,)),
            dma((2, 2, 4, 4)),
            dma((2, 2, 4, 4)),
        ],
        compiler_params=pltpu.CompilerParams(
            collective_id=0, has_side_effects=True, vmem_limit_bytes=56 * 2**20
        ),
        cost_estimate=pl.CostEstimate(flops=5 * 10**9, bytes_accessed=4 * 10**6, transcendentals=6 * 10**6),
    )(unit_slot.reshape(1, -1), unit_doc.reshape(1, -1), queries, key_value_rows)


def solution(mesh):
    in_specs = (P(("ctx", "grp"), None), P(("ctx", "grp"), None), P(), P())
    out_specs = P(("ctx", "grp"), None)
    return jax.shard_map(local, mesh=mesh, in_specs=in_specs, out_specs=out_specs, check_vma=False)
```
